32 devices in a mesh: groups: 2 (over x), pair: 16 (over z, y, core).
Axes of the slice: x: 2, y: 2, z: 4, core: 2. Of those that a mesh axis runs over, the one named last changes fastest.
Arguments:
- integrals: bfloat16 [6144, 2048], P('pair'), may hold values from -0.078125 to 0.078125
- probes: bfloat16 [12288, 128], P(('groups', 'pair')), parts along dimension 0, may hold values from -6 to 6
- occ_energy: float32 [8000], replicated, may hold values from -1.4 to -0.3
- vir_energy: float32 [32000], replicated, may hold values from 0.02 to 3
- block_occ: int32 [16], P('pair'), may hold values from 0 to 7999
- block_vir: int32 [16], P('pair'), may hold values from 0 to 249
- block_count: int32 [16], P('pair'), may hold values from 1 to 128, 1024 in all
- frequency: float32 [2], P('groups'), parts along dimension 0, may hold values from 0.1 to 2
Outputs:
- images: float32 [12288, 128], P(('groups', 'pair')), parts along dimension 0
The draws below stay inside these ranges and needn't reach their ends.
There are 2 independent parts, one for each index of `groups`. The reference program is written for one: setup_inputs(seed, part) draws one part's arguments, and reference() takes and returns one part's arrays. A program takes and returns all parts, laid end to end along the dimension named above; an argument that names none is the same for every part. Nothing has to cross between parts.
Inputs may be any that keep to these rules, and one draw needn't show every extreme that they name: `block_count`: columns at and after a slot's count are padding; some slot has all 128 columns live.
All inputs are finite; a program needn't handle non-finite values. No bound on the sum of `block_count` on one device may be relied on, other than what follows from the above.
Results may differ from the reference program's by a relative error of at most 0.00051.
Values may be sent and summed in bfloat16 or wider, within the bound.
A program may use at most 64 MiB of HBM per device.

```python
import math
import jax
import jax.numpy as jnp
import numpy as np

NOCC = 8000
NVIR = 32000
NPROBE = 128
NAUX = 6144
NBLK = 16


def set_ends(array, key, least, largest):
    spot = [jax.random.randint(jax.random.fold_in(key, axis), (), 0, length) for axis, length in enumerate(array.shape)]
    longest = array.shape.index(max(array.shape))
    beside = spot[:longest] + [(spot[longest] + 1) % array.shape[longest]] + spot[longest + 1:]
    return array.at[tuple(spot)].set(least).at[tuple(beside)].set(largest)


def levels(own_key, shape, pieces, smallest, high):
    loudness, own = 1.0, jax.random.fold_in(own_key, 6)
    for axis_at, blocks in pieces:
        draws = jnp.exp(jax.random.uniform(jax.random.fold_in(own, axis_at), (blocks,), jnp.float32, smallest / len(pieces), high / len(pieces)))
        loudness = loudness * jnp.repeat(draws, shape[axis_at] // blocks).reshape([-1 if axis == axis_at else 1 for axis in range(len(shape))])
    return loudness


def split_up(count, total, reach, slope):
    portions = [(1 << 20) // math.isqrt(standing ** slope) + 1 for standing in range(2, count + 1)]
    surplus, given = total - reach - (count - 1), [1] * (count - 1)
    while surplus > 0:
        movable = [i for i in range(count - 1) if given[i] < reach]
        mass, remaining = sum([portions[i] for i in movable]), surplus
        for i in movable:
            more = min(reach - given[i], max(1, remaining * portions[i] // mass), surplus)
            given[i] = given[i] + more
            surplus = surplus - more
    return np.array([reach] + given)


def ragged_sizes(rng, amount, total, most, slope):
    if amount == 2:
        one = jax.random.randint(rng, (), max(1, total - most), min(most, total - 1) + 1)
        return jnp.stack([one, total - one])
    lengths = jnp.asarray(split_up(amount, total, most, slope), jnp.int32)
    twos = (amount - 1) // 2
    giver, taker = lengths[1:1 + 2 * twos:2], lengths[2:2 + 2 * twos:2]
    margin = jnp.minimum(giver - 1, most - taker)
    passed = jax.random.randint(jax.random.fold_in(rng, 1), (twos,), 0, 1 << 20) % (margin + 1)
    lengths = lengths.at[1:1 + 2 * twos:2].set(giver - passed).at[2:2 + 2 * twos:2].set(taker + passed)
    return lengths[jax.random.permutation(jax.random.fold_in(rng, 2), amount)]


def scatter_about(key, dims, scale, limit, split=(), kind=jnp.bfloat16):
    entries = jax.random.normal(key, dims, jnp.float32) * scale
    if len(split) > 0:
        entries = levels(key, dims, split, -0.22, 0.18) * entries
    return jnp.clip(entries, min=-limit, max=limit).astype(kind)


def setup_inputs(seed: int = 0, part: int = 0) -> dict:
    arg_keys = jax.random.split(jax.random.key(seed), 9)
    part_splits = jax.random.split(jax.random.fold_in(arg_keys[8], part), 9)
    return {
        "integrals": scatter_about(arg_keys[0], (NAUX, NBLK * 128), NAUX ** -0.5, 0.078125, ((0, 16),)),
        "probes": scatter_about(part_splits[1], (NAUX, NPROBE), 1.0, 6.0, ((0, 16),)),
        "occ_energy": jnp.clip(jax.random.uniform(arg_keys[2], (NOCC,), jnp.float32, -1.4, -0.3), -1.4, -0.3),
        "vir_energy": jnp.clip(jax.random.uniform(arg_keys[3], (NVIR,), jnp.float32, 0.02, 3.0), 0.02, 3.0),
        "block_occ": set_ends(jax.random.randint(arg_keys[4], (NBLK,), 0, NOCC), jax.random.fold_in(arg_keys[4], 1), 0, NOCC - 1).astype(jnp.int32),
        "block_vir": set_ends(jax.random.randint(arg_keys[5], (NBLK,), 0, NVIR // 128), jax.random.fold_in(arg_keys[5], 1), 0, (NVIR // 128) - 1).astype(jnp.int32),
        "block_count": ragged_sizes(arg_keys[6], NBLK, NBLK * 64, 128, 2).astype(jnp.int32),
        "frequency": jnp.clip(jnp.exp(jax.random.uniform(part_splits[7], (1,), jnp.float32, math.log(0.1), math.log(2.0))), 0.1, 2.0),
    }


def reference(integrals, probes, occ_energy, vir_energy, block_occ, block_vir, block_count, frequency):
    column_index = jnp.arange(128, dtype=jnp.int32)
    live_cols = column_index[None, :] < block_count[:, None]
    vir_rows = vir_energy.reshape(NVIR // 128, 128)[block_vir]
    energy_gap = vir_rows - occ_energy[block_occ][:, None]
    omega_val = frequency[0]
    ratio = 2.0 * energy_gap / (energy_gap * energy_gap + omega_val * omega_val)
    weights = jnp.where(live_cols, ratio, jnp.zeros_like(ratio)).reshape(-1)
    projected = jnp.dot(integrals.T, probes, preferred_element_type=jnp.float32)
    weighted = (projected * weights[:, None]).astype(jnp.bfloat16)
    return jnp.dot(integrals, weighted, preferred_element_type=jnp.float32)
```

```python
import functools

import jax
import jax.numpy as jnp
from jax import lax
from jax.experimental import pallas as pl
from jax.experimental.pallas import tpu as pltpu
from jax.sharding import PartitionSpec as P

LANES = 128


def kernel(
    nz, ny, integ_hbm, probes_hbm, vir_hbm, occ_ref, bocc_ref, bvir_ref, bcount_ref, freq_ref,
    out_ref,
    integ, probes, vir, partial, r1, r2, r3, gathered,
    in_sem, s1, v1, s2, v2, s3, v3, gzs, gzv, gys, gyv, gcs, gcv,
):
    nq = nz * ny
    me = lax.axis_index("pair")
    c = lax.rem(me, 2)
    q_me = me // 2
    y = lax.rem(q_me, ny)
    z = q_me // ny
    wide = 2 * LANES

    def dev(zz, yy, cc):
        return {"pair": (zz * ny + yy) * 2 + cc}

    mate = dev(z, y, 1 - c)
    ymate = dev(z, ny - 1 - y, c)

    def remote(src, dst, ss, rs, where):
        return pltpu.make_async_remote_copy(
            src_ref=src, dst_ref=dst, send_sem=ss, recv_sem=rs,
            device_id=where, device_id_type=pl.DeviceIdType.MESH,
        )

    loads = [pltpu.make_async_copy(probes_hbm, probes, in_sem.at[nq])]
    for q in range(nq):
        cols = pl.ds(q * wide, wide)
        loads.append(pltpu.make_async_copy(integ_hbm.at[:, cols], integ.at[:, cols], in_sem.at[q]))
    loads.append(pltpu.make_async_copy(vir_hbm, vir, in_sem.at[nq + 1]))
    for load in loads:
        load.start()

    barrier = pltpu.get_barrier_semaphore()
    peers = [mate] + ([ymate] if ny > 1 else [])
    peers += [dev(lax.rem(z + d, nz), y, c) for d in range(1, nz)]
    for peer in peers:
        pl.semaphore_signal(barrier, inc=1, device_id=peer, device_id_type=pl.DeviceIdType.MESH)

    sends = []
    loads[0].wait()
    for q in range(nq):
        loads[1 + q].wait()
        block = lax.dot_general(
            integ[:, q * wide:(q + 1) * wide], probes[...], (((0,), (0,)), ((), ())),
            preferred_element_type=jnp.float32,
        )
        partial[q] = block.reshape(2, LANES, LANES)
        if q == 0:
            pl.semaphore_wait(barrier, len(peers))
        copy = remote(partial.at[q, 1 - c], r1.at[q], s1.at[q], v1.at[q], mate)
        copy.start()
        sends.append(copy)
    core_copies = list(sends)

    loads[-1].wait()
    gap = vir[pl.ds(bvir_ref[0], 1), :] - occ_ref[bocc_ref[0]]
    omega = freq_ref[0]
    ratio = 2.0 * gap / (gap * gap + omega * omega)
    lane = lax.broadcasted_iota(jnp.int32, (1, LANES), 1)
    ratio = jnp.where(lane < bcount_ref[0], ratio, jnp.zeros_like(ratio))
    weights = jnp.transpose(jnp.broadcast_to(ratio, (LANES, LANES)))

    for q in range(nq):
        core_copies[q].wait_recv()

    order = [lax.rem(z + d, nz) for d in range(1, nz)] + [z]
    y_copies = []
    if ny > 1:
        for zz in order:
            qq = zz * ny + (ny - 1 - y)
            partial[qq, c] = partial[qq, c] + r1[qq]
            copy = remote(partial.at[qq, c], r2.at[zz], s2.at[zz], v2.at[zz], ymate)
            copy.start()
            y_copies.append(copy)
        sends += y_copies
    for d, zz in enumerate(order[:-1]):
        qq = zz * ny + y
        total = partial[qq, c] + r1[qq]
        if ny > 1:
            y_copies[d].wait_recv()
            total = total + r2[zz]
        partial[qq, c] = total
        copy = remote(partial.at[qq, c], r3.at[z], s3.at[zz], v3.at[z], dev(zz, y, c))
        copy.start()
        sends.append(copy)
    total = partial[q_me, c] + r1[q_me]
    if ny > 1:
        y_copies[-1].wait_recv()
        total = total + r2[z]
    for d in range(1, nz):
        zs = lax.rem(z + nz - d, nz)
        remote(r3.at[zs], r3.at[zs], s3.at[zs], v3.at[zs], dev(zs, y, c)).wait_recv()
        total = total + r3[zs]
    gathered[me] = (total * weights).astype(jnp.bfloat16)

    def spread(zs, yy):
        j = (zs * ny + yy) * 2 + c
        if True:
            copy = remote(gathered.at[j], gathered.at[j], gcs.at[j // 2], gcv.at[j // 2], mate)
            copy.start()
            sends.append(copy)

    def to_y(zs):
        j = (zs * ny + y) * 2 + c
        copy = remote(gathered.at[j], gathered.at[j], gys.at[zs], gyv.at[zs], ymate)
        copy.start()
        sends.append(copy)

    for d in range(1, nz):
        zz = lax.rem(z + d, nz)
        copy = remote(gathered.at[me], gathered.at[me], gzs.at[zz], gzv.at[z], dev(zz, y, c))
        copy.start()
        sends.append(copy)
    if ny > 1:
        to_y(z)
    spread(z, y)
    arrivals = [z]
    for d in range(1, nz):
        zs = lax.rem(z + nz - d, nz)
        arrivals.append(zs)
        j = (zs * ny + y) * 2 + c
        remote(gathered.at[j], gathered.at[j], gzs.at[zs], gzv.at[zs], dev(zs, y, c)).wait_recv()
        if ny > 1:
            to_y(zs)
        spread(zs, y)
    if ny > 1:
        for zs in arrivals:
            j = (zs * ny + (ny - 1 - y)) * 2 + c
            remote(gathered.at[j], gathered.at[j], gys.at[zs], gyv.at[zs], ymate).wait_recv()
            spread(zs, ny - 1 - y)

    group = ny * 2 * LANES
    for n, zs in enumerate(arrivals):
        for yy in range(ny):
            q = zs * ny + yy
            j = q * 2 + 1 - c
            remote(gathered.at[j], gathered.at[j], gcs.at[q], gcv.at[q], mate).wait_recv()
        rows = gathered[pl.ds(zs * ny * 2, ny * 2)].reshape(group, LANES)
        cols = pl.ds(pl.multiple_of(zs * group, group), group)
        term = jnp.dot(integ[:, cols], rows, preferred_element_type=jnp.float32)
        if n == 0:
            out_ref[...] = term
        else:
            out_ref[...] += term
    for copy in sends:
        copy.wait_send()


def solution(mesh):
    npair = mesh.shape["pair"]
    ny = 2 if npair == 16 else 1
    nz = npair // 2 // ny

    def on_device(integrals, probes, occ, vir, bocc, bvir, bcount, freq):
        aux, ncol = integrals.shape
        nq = nz * ny
        f32, bf16 = jnp.float32, jnp.bfloat16
        vir = vir.reshape(-1, LANES)
        dma = pltpu.SemaphoreType.DMA
        smem = pl.BlockSpec(memory_space=pltpu.SMEM)
        hbm = pl.BlockSpec(memory_space=pl.ANY)
        tile = (LANES, LANES)
        return pl.pallas_call(
            functools.partial(kernel, nz, ny),
            out_shape=jax.ShapeDtypeStruct((aux, LANES), f32),
            in_specs=[hbm, hbm, hbm] + [smem] * 5,
            out_specs=pl.BlockSpec(memory_space=pltpu.VMEM),
            scratch_shapes=[
                pltpu.VMEM((aux, ncol), bf16),
                pltpu.VMEM((aux, LANES), bf16),
                pltpu.VMEM(vir.shape, f32),
                pltpu.VMEM((nq, 2) + tile, f32),
                pltpu.VMEM((nq,) + tile, f32),
                pltpu.VMEM((nz,) + tile, f32),
                pltpu.VMEM((nz,) + tile, f32),
                pltpu.VMEM((npair,) + tile, bf16),
                dma((nq + 2,)),
                dma((nq,)), dma((nq,)),
                dma((nz,)), dma((nz,)),
                dma((nz,)), dma((nz,)),
                dma((nz,)), dma((nz,)),
                dma((nz,)), dma((nz,)),
                dma((nq,)), dma((nq,)),
            ],
            compiler_params=pltpu.CompilerParams(
                collective_id=0, has_side_effects=True, vmem_limit_bytes=40 * 1024 * 1024
            ),
            cost_estimate=pl.CostEstimate(
                flops=4 * aux * ncol * LANES, bytes_accessed=2 * aux * ncol, transcendentals=0
            ),
        )(integrals, probes, vir, occ, bocc, bvir, bcount, freq)

    in_specs = (
        P("pair", None), P(("groups", "pair"), None), P(), P(),
        P("pair"), P("pair"), P("pair"), P("groups"),
    )
    return jax.shard_map(
        on_device, mesh=mesh, in_specs=in_specs,
        out_specs=P(("groups", "pair"), None), check_vma=False,
    )
```

```python
import functools

import jax
import jax.numpy as jnp
from jax import lax
from jax.experimental import pallas as pl
from jax.experimental.pallas import tpu as pltpu
from jax.sharding import PartitionSpec as P

LANES = 128


def kernel(
    nz, ny, integ_hbm, probes_hbm, vir_hbm, occ_hbm, bocc_hbm, bvir_hbm, bcount_hbm, freq_hbm,
    out_ref,
    integ, probes, vir, occ, bocc_ref, bvir_ref, bcount_ref, freq_ref, partial, r1, r2, r3, gathered,
    in_sem, s1, v1, s2, v2, s3, v3, gzs, gzv, gys, gyv, gcs, gcv,
):
    nq = nz * ny
    me = lax.axis_index("pair")
    c = lax.rem(me, 2)
    q_me = me // 2
    y = lax.rem(q_me, ny)
    z = q_me // ny
    wide = 2 * LANES

    def dev(zz, yy, cc):
        return {"pair": (zz * ny + yy) * 2 + cc}

    mate = dev(z, y, 1 - c)
    ymate = dev(z, ny - 1 - y, c)

    def remote(src, dst, ss, rs, where):
        return pltpu.make_async_remote_copy(
            src_ref=src, dst_ref=dst, send_sem=ss, recv_sem=rs,
            device_id=where, device_id_type=pl.DeviceIdType.MESH,
        )

    loads = [pltpu.make_async_copy(probes_hbm, probes, in_sem.at[nq])]
    for q in range(nq):
        cols = pl.ds(q * wide, wide)
        loads.append(pltpu.make_async_copy(integ_hbm.at[:, cols], integ.at[:, cols], in_sem.at[q]))
    loads.append(pltpu.make_async_copy(vir_hbm, vir, in_sem.at[nq + 1]))
    small = (
        (occ_hbm, occ), (bocc_hbm, bocc_ref), (bvir_hbm, bvir_ref),
        (bcount_hbm, bcount_ref), (freq_hbm, freq_ref),
    )
    for n, (src, dst) in enumerate(small):
        loads.append(pltpu.make_async_copy(src, dst, in_sem.at[nq + 2 + n]))
    for load in loads:
        load.start()

    barrier = pltpu.get_barrier_semaphore()
    peers = [mate] + ([ymate] if ny > 1 else [])
    peers += [dev(lax.rem(z + d, nz), y, c) for d in range(1, nz)]
    for peer in peers:
        pl.semaphore_signal(barrier, inc=1, device_id=peer, device_id_type=pl.DeviceIdType.MESH)

    sends = []
    loads[0].wait()
    for q in range(nq):
        loads[1 + q].wait()
        block = lax.dot_general(
            integ[:, q * wide:(q + 1) * wide], probes[...], (((0,), (0,)), ((), ())),
            preferred_element_type=jnp.float32,
        )
        partial[q] = block.reshape(2, LANES, LANES)
        if q == 0:
            pl.semaphore_wait(barrier, len(peers))
        copy = remote(partial.at[q, 1 - c], r1.at[q], s1.at[q], v1.at[q], mate)
        copy.start()
        sends.append(copy)
    core_copies = list(sends)

    for load in loads[1 + nq:]:
        load.wait()
    gap = vir[pl.ds(bvir_ref[0], 1), :] - occ[bocc_ref[0]]
    omega = freq_ref[0]
    ratio = 2.0 * gap / (gap * gap + omega * omega)
    lane = lax.broadcasted_iota(jnp.int32, (1, LANES), 1)
    ratio = jnp.where(lane < bcount_ref[0], ratio, jnp.zeros_like(ratio))
    weights = jnp.transpose(jnp.broadcast_to(ratio, (LANES, LANES)))

    for q in range(nq):
        core_copies[q].wait_recv()

    order = [lax.rem(z + d, nz) for d in range(1, nz)] + [z]
    y_copies = []
    if ny > 1:
        for zz in order:
            qq = zz * ny + (ny - 1 - y)
            partial[qq, c] = partial[qq, c] + r1[qq]
            copy = remote(partial.at[qq, c], r2.at[zz], s2.at[zz], v2.at[zz], ymate)
            copy.start()
            y_copies.append(copy)
        sends += y_copies
    for d, zz in enumerate(order[:-1]):
        qq = zz * ny + y
        total = partial[qq, c] + r1[qq]
        if ny > 1:
            y_copies[d].wait_recv()
            total = total + r2[zz]
        partial[qq, c] = total
        copy = remote(partial.at[qq, c], r3.at[z], s3.at[zz], v3.at[z], dev(zz, y, c))
        copy.start()
        sends.append(copy)
    total = partial[q_me, c] + r1[q_me]
    if ny > 1:
        y_copies[-1].wait_recv()
        total = total + r2[z]
    for d in range(1, nz):
        zs = lax.rem(z + nz - d, nz)
        remote(r3.at[zs], r3.at[zs], s3.at[zs], v3.at[zs], dev(zs, y, c)).wait_recv()
        total = total + r3[zs]
    gathered[me] = (total * weights).astype(jnp.bfloat16)

    def spread(zs, yy):
        j = (zs * ny + yy) * 2 + c
        copy = remote(gathered.at[j], gathered.at[j], gcs.at[j // 2], gcv.at[j // 2], mate)
        copy.start()
        sends.append(copy)

    def to_y(zs):
        j = (zs * ny + y) * 2 + c
        copy = remote(gathered.at[j], gathered.at[j], gys.at[zs], gyv.at[zs], ymate)
        copy.start()
        sends.append(copy)

    for d in range(1, nz):
        zz = lax.rem(z + d, nz)
        copy = remote(gathered.at[me], gathered.at[me], gzs.at[zz], gzv.at[z], dev(zz, y, c))
        copy.start()
        sends.append(copy)
    if ny > 1:
        to_y(z)
    spread(z, y)
    arrivals = [z]
    for d in range(1, nz):
        zs = lax.rem(z + nz - d, nz)
        arrivals.append(zs)
        j = (zs * ny + y) * 2 + c
        remote(gathered.at[j], gathered.at[j], gzs.at[zs], gzv.at[zs], dev(zs, y, c)).wait_recv()
        if ny > 1:
            to_y(zs)
        spread(zs, y)
    if ny > 1:
        for zs in arrivals:
            j = (zs * ny + (ny - 1 - y)) * 2 + c
            remote(gathered.at[j], gathered.at[j], gys.at[zs], gyv.at[zs], ymate).wait_recv()
            spread(zs, ny - 1 - y)

    group = ny * 2 * LANES
    for n, zs in enumerate(arrivals):
        for yy in range(ny):
            q = zs * ny + yy
            j = q * 2 + 1 - c
            remote(gathered.at[j], gathered.at[j], gcs.at[q], gcv.at[q], mate).wait_recv()
        rows = gathered[pl.ds(zs * ny * 2, ny * 2)].reshape(group, LANES)
        cols = pl.ds(pl.multiple_of(zs * group, group), group)
        term = jnp.dot(integ[:, cols], rows, preferred_element_type=jnp.float32)
        if n == 0:
            out_ref[...] = term
        else:
            out_ref[...] += term
    for copy in sends:
        copy.wait_send()


def solution(mesh):
    npair = mesh.shape["pair"]
    ny = 2 if npair == 16 else 1
    nz = npair // 2 // ny

    def on_device(integrals, probes, occ, vir, bocc, bvir, bcount, freq):
        aux, ncol = integrals.shape
        nq = nz * ny
        f32, bf16 = jnp.float32, jnp.bfloat16
        vir = vir.reshape(-1, LANES)
        dma = pltpu.SemaphoreType.DMA
        hbm = pl.BlockSpec(memory_space=pltpu.HBM)
        tile = (LANES, LANES)
        return pl.pallas_call(
            functools.partial(kernel, nz, ny),
            out_shape=jax.ShapeDtypeStruct((aux, LANES), f32),
            in_specs=[hbm] * 8,
            out_specs=pl.BlockSpec(memory_space=pltpu.VMEM),
            scratch_shapes=[
                pltpu.VMEM((aux, ncol), bf16),
                pltpu.VMEM((aux, LANES), bf16),
                pltpu.VMEM(vir.shape, f32),
                pltpu.SMEM(occ.shape, f32),
                pltpu.SMEM((1,), jnp.int32), pltpu.SMEM((1,), jnp.int32), pltpu.SMEM((1,), jnp.int32),
                pltpu.SMEM((1,), f32),
                pltpu.VMEM((nq, 2) + tile, f32),
                pltpu.VMEM((nq,) + tile, f32),
                pltpu.VMEM((nz,) + tile, f32),
                pltpu.VMEM((nz,) + tile, f32),
                pltpu.VMEM((npair,) + tile, bf16),
                dma((nq + 7,)),
                dma((nq,)), dma((nq,)),
                dma((nz,)), dma((nz,)),
                dma((nz,)), dma((nz,)),
                dma((nz,)), dma((nz,)),
                dma((nz,)), dma((nz,)),
                dma((nq,)), dma((nq,)),
            ],
            compiler_params=pltpu.CompilerParams(
                collective_id=0, has_side_effects=True, vmem_limit_bytes=63 * 1024 * 1024
            ),
            cost_estimate=pl.CostEstimate(
                flops=4 * aux * ncol * LANES, bytes_accessed=2 * aux * ncol, transcendentals=0
            ),
        )(integrals, probes, vir, occ, bocc, bvir, bcount, freq)

    in_specs = (
        P("pair", None), P(("groups", "pair"), None), P(), P(),
        P("pair"), P("pair"), P("pair"), P("groups"),
    )
    return jax.shard_map(
        on_device, mesh=mesh, in_specs=in_specs,
        out_specs=P(("groups", "pair"), None), check_vma=False,
    )
```

```python
import functools

import jax
import jax.numpy as jnp
from jax import lax
from jax.experimental import pallas as pl
from jax.experimental.pallas import tpu as pltpu
from jax.sharding import PartitionSpec as P

LANES = 128
RS_PARTS = 2
AG_PARTS = 2


def kernel(
    nz, ny, integ_hbm, probes_hbm, vir_hbm, occ_hbm, bocc_hbm, bvir_hbm, bcount_hbm, freq_hbm,
    out_ref,
    integ, probes, vir, occ, bocc_ref, bvir_ref, bcount_ref, freq_ref, partial, r1, r2, r3, gathered,
    in_sem, s1, v1, s2, v2, s3, v3, gzs, gzv, gys, gyv, gcs, gcv,
):
    nq = nz * ny
    me = lax.axis_index("pair")
    c = lax.rem(me, 2)
    q_me = me // 2
    y = lax.rem(q_me, ny)
    z = q_me // ny
    wide = 2 * LANES

    def dev(zz, yy, cc):
        return {"pair": (zz * ny + yy) * 2 + cc}

    mate = dev(z, y, 1 - c)
    ymate = dev(z, ny - 1 - y, c)

    def remote(src, dst, ss, rs, where):
        return pltpu.make_async_remote_copy(
            src_ref=src, dst_ref=dst, send_sem=ss, recv_sem=rs,
            device_id=where, device_id_type=pl.DeviceIdType.MESH,
        )

    order = [lax.rem(z + d, nz) for d in range(1, nz)] + [z]
    blocks = [zz * ny + (ny - 1 - y) for zz in order] if ny > 1 else []
    blocks += [zz * ny + y for zz in order]

    def columns(q):
        return pl.ds(pl.multiple_of(q * wide, wide), wide)

    loads = [pltpu.make_async_copy(probes_hbm, probes, in_sem.at[nq])]
    for k, q in enumerate(blocks):
        loads.append(
            pltpu.make_async_copy(integ_hbm.at[:, columns(q)], integ.at[:, columns(q)], in_sem.at[k])
        )
    loads.append(pltpu.make_async_copy(vir_hbm, vir, in_sem.at[nq + 1]))
    small = (
        (occ_hbm, occ), (bocc_hbm, bocc_ref), (bvir_hbm, bvir_ref),
        (bcount_hbm, bcount_ref), (freq_hbm, freq_ref),
    )
    for n, (src, dst) in enumerate(small):
        loads.append(pltpu.make_async_copy(src, dst, in_sem.at[nq + 2 + n]))
    for load in loads:
        load.start()

    barrier = pltpu.get_barrier_semaphore()
    peers = [mate] + ([ymate] if ny > 1 else [])
    peers += [dev(lax.rem(z + d, nz), y, c) for d in range(1, nz)]
    for peer in peers:
        pl.semaphore_signal(barrier, inc=1, device_id=peer, device_id_type=pl.DeviceIdType.MESH)

    sends = []
    core_copies = []
    y_copies = []

    def to_mate(k, q):
        loads[1 + k].wait()
        block = lax.dot_general(
            integ[:, columns(q)], probes[...], (((0,), (0,)), ((), ())),
            preferred_element_type=jnp.float32,
        )
        partial[q] = block.reshape(2, RS_PARTS, LANES // RS_PARTS, LANES)
        if k == 0:
            pl.semaphore_wait(barrier, len(peers))
        copy = remote(partial.at[q, 1 - c], r1.at[q], s1.at[k], v1.at[k], mate)
        copy.start()
        sends.append(copy)
        core_copies.append(copy)

    def to_ymate(k):
        q, zz = blocks[k], order[k]
        core_copies[k].wait_recv()
        for h in range(RS_PARTS):
            partial[q, c, h] = partial[q, c, h] + r1[q, h]
            copy = remote(partial.at[q, c, h], r2.at[zz, h], s2.at[k, h], v2.at[k, h], ymate)
            copy.start()
            sends.append(copy)
            y_copies.append(copy)

    loads[0].wait()
    lag = 3
    n_y = nz if ny > 1 else 0
    for k, q in enumerate(blocks):
        to_mate(k, q)
        if 0 <= k - lag < n_y:
            to_ymate(k - lag)
    for k in range(max(0, nq - lag), n_y):
        to_ymate(k)

    for load in loads[1 + nq:]:
        load.wait()
    gap = vir[pl.ds(bvir_ref[0], 1), :] - occ[bocc_ref[0]]
    omega = freq_ref[0]
    ratio = 2.0 * gap / (gap * gap + omega * omega)
    lane = lax.broadcasted_iota(jnp.int32, (1, LANES), 1)
    ratio = jnp.where(lane < bcount_ref[0], ratio, jnp.zeros_like(ratio))
    weights = jnp.transpose(jnp.broadcast_to(ratio, (LANES, LANES)))

    for d, zz in enumerate(order[:-1]):
        q = blocks[n_y + d]
        core_copies[n_y + d].wait_recv()
        for h in range(RS_PARTS):
            total = partial[q, c, h] + r1[q, h]
            if ny > 1:
                y_copies[d * RS_PARTS + h].wait_recv()
                total = total + r2[zz, h]
            partial[q, c, h] = total
            copy = remote(partial.at[q, c, h], r3.at[z, h], s3.at[d, h], v3.at[z, h], dev(zz, y, c))
            copy.start()
            sends.append(copy)
    core_copies[-1].wait_recv()
    rows_r = LANES // RS_PARTS
    rows_a = LANES // AG_PARTS

    def to_z(h):
        for d in range(1, nz):
            zz = lax.rem(z + d, nz)
            copy = remote(
                gathered.at[me, h], gathered.at[me, h], gzs.at[zz, h], gzv.at[z, h], dev(zz, y, c)
            )
            copy.start()
            sends.append(copy)

    def to_y(zs, h):
        j = (zs * ny + y) * 2 + c
        copy = remote(gathered.at[j, h], gathered.at[j, h], gys.at[zs, h], gyv.at[zs, h], ymate)
        copy.start()
        sends.append(copy)

    def spread(zs, yy, h):
        j = (zs * ny + yy) * 2 + c
        q = zs * ny + yy
        copy = remote(gathered.at[j, h], gathered.at[j, h], gcs.at[q, h], gcv.at[q, h], mate)
        copy.start()
        sends.append(copy)

    done = 0
    for h in range(RS_PARTS):
        total = partial[q_me, c, h] + r1[q_me, h]
        if ny > 1:
            y_copies[(nz - 1) * RS_PARTS + h].wait_recv()
            total = total + r2[z, h]
        for d in range(1, nz):
            zs = lax.rem(z + nz - d, nz)
            remote(
                r3.at[zs, h], r3.at[zs, h], s3.at[d - 1, h], v3.at[zs, h], dev(zs, y, c)
            ).wait_recv()
            total = total + r3[zs, h]
        value = (total * weights[h * rows_r:(h + 1) * rows_r]).astype(jnp.bfloat16)
        if rows_a <= rows_r:
            per = rows_r // rows_a
            for g in range(per):
                gathered[me, h * per + g] = value[g * rows_a:(g + 1) * rows_a]
        else:
            per = rows_a // rows_r
            gathered[me, h // per, (h % per) * rows_r:(h % per + 1) * rows_r] = value
        while (done + 1) * rows_a <= (h + 1) * rows_r:
            to_z(done)
            if ny > 1:
                to_y(z, done)
            spread(z, y, done)
            done += 1
    arrivals = [z] + [lax.rem(z + nz - d, nz) for d in range(1, nz)]
    for h in range(AG_PARTS):
        for zs in arrivals[1:]:
            j = (zs * ny + y) * 2 + c
            remote(
                gathered.at[j, h], gathered.at[j, h], gzs.at[zs, h], gzv.at[zs, h], dev(zs, y, c)
            ).wait_recv()
            if ny > 1:
                to_y(zs, h)
            spread(zs, y, h)
    if ny > 1:
        for h in range(AG_PARTS):
            for zs in arrivals:
                j = (zs * ny + (ny - 1 - y)) * 2 + c
                remote(
                    gathered.at[j, h], gathered.at[j, h], gys.at[zs, h], gyv.at[zs, h], ymate
                ).wait_recv()
                spread(zs, ny - 1 - y, h)

    group = ny * 2 * LANES
    for n, zs in enumerate(arrivals):
        for yy in range(ny):
            q = zs * ny + yy
            j = q * 2 + 1 - c
            for h in range(AG_PARTS):
                remote(
                    gathered.at[j, h], gathered.at[j, h], gcs.at[q, h], gcv.at[q, h], mate
                ).wait_recv()
        rows = gathered[pl.ds(zs * ny * 2, ny * 2)].reshape(group, LANES)
        cols = pl.ds(pl.multiple_of(zs * group, group), group)
        term = jnp.dot(integ[:, cols], rows, preferred_element_type=jnp.float32)
        if n == 0:
            out_ref[...] = term
        else:
            out_ref[...] += term
    for copy in sends:
        copy.wait_send()


def solution(mesh):
    npair = mesh.shape["pair"]
    ny = 2 if npair == 16 else 1
    nz = npair // 2 // ny

    def on_device(integrals, probes, occ, vir, bocc, bvir, bcount, freq):
        aux, ncol = integrals.shape
        nq = nz * ny
        f32, bf16 = jnp.float32, jnp.bfloat16
        vir = vir.reshape(-1, LANES)
        dma = pltpu.SemaphoreType.DMA
        hbm = pl.BlockSpec(memory_space=pltpu.HBM)
        tile_r = (RS_PARTS, LANES // RS_PARTS, LANES)
        tile_a = (AG_PARTS, LANES // AG_PARTS, LANES)
        return pl.pallas_call(
            functools.partial(kernel, nz, ny),
            out_shape=jax.ShapeDtypeStruct((aux, LANES), f32),
            in_specs=[hbm] * 8,
            out_specs=pl.BlockSpec(memory_space=pltpu.VMEM),
            scratch_shapes=[
                pltpu.VMEM((aux, ncol), bf16),
                pltpu.VMEM((aux, LANES), bf16),
                pltpu.VMEM(vir.shape, f32),
                pltpu.SMEM(occ.shape, f32),
                pltpu.SMEM((1,), jnp.int32), pltpu.SMEM((1,), jnp.int32), pltpu.SMEM((1,), jnp.int32),
                pltpu.SMEM((1,), f32),
                pltpu.VMEM((nq, 2) + tile_r, f32),
                pltpu.VMEM((nq,) + tile_r, f32),
                pltpu.VMEM((nz,) + tile_r, f32),
                pltpu.VMEM((nz,) + tile_r, f32),
                pltpu.VMEM((npair,) + tile_a, bf16),
                dma((nq + 7,)),
                dma((nq,)), dma((nq,)),
                dma((nz, RS_PARTS)), dma((nz, RS_PARTS)),
                dma((nz, RS_PARTS)), dma((nz, RS_PARTS)),
                dma((nz, AG_PARTS)), dma((nz, AG_PARTS)),
                dma((nz, AG_PARTS)), dma((nz, AG_PARTS)),
                dma((nq, AG_PARTS)), dma((nq, AG_PARTS)),
            ],
            compiler_params=pltpu.CompilerParams(
                collective_id=0, has_side_effects=True, vmem_limit_bytes=63 * 1024 * 1024
            ),
            cost_estimate=pl.CostEstimate(
                flops=4 * aux * ncol * LANES, bytes_accessed=2 * aux * ncol, transcendentals=0
            ),
        )(integrals, probes, vir, occ, bocc, bvir, bcount, freq)

    in_specs = (
        P("pair", None), P(("groups", "pair"), None), P(), P(),
        P("pair"), P("pair"), P("pair"), P("groups"),
    )
    return jax.shard_map(
        on_device, mesh=mesh, in_specs=in_specs,
        out_specs=P(("groups", "pair"), None), check_vma=False,
    )
```

```python
import functools

import jax
import jax.numpy as jnp
from jax import lax
from jax.experimental import pallas as pl
from jax.experimental.pallas import tpu as pltpu
from jax.sharding import PartitionSpec as P

LANES = 128
RS_PARTS = 2
AG_PARTS = 2


def kernel(
    nz, ny, integ_hbm, probes_hbm, vir_hbm, occ_hbm, bocc_hbm, bvir_hbm, bcount_hbm, freq_hbm,
    out_ref,
    integ, probes, vir, occ, bocc_ref, bvir_ref, bcount_ref, freq_ref, partial, r1, r2, r3, gathered,
    in_sem, s1, v1, s2, v2, s3, v3, gzs, gzv, gys, gyv, gcs, gcv,
):
    nq = nz * ny
    rs_steps = sorted(range(1, nz), key=lambda d: abs(2 * d - nz))
    ag_steps = sorted(range(1, nz), key=lambda d: abs(2 * d - nz))
    me = lax.axis_index("pair")
    c = lax.rem(me, 2)
    q_me = me // 2
    y = lax.rem(q_me, ny)
    z = q_me // ny
    wide = 2 * LANES

    def dev(zz, yy, cc):
        return {"pair": (zz * ny + yy) * 2 + cc}

    mate = dev(z, y, 1 - c)
    ymate = dev(z, ny - 1 - y, c)

    def remote(src, dst, ss, rs, where):
        return pltpu.make_async_remote_copy(
            src_ref=src, dst_ref=dst, send_sem=ss, recv_sem=rs,
            device_id=where, device_id_type=pl.DeviceIdType.MESH,
        )

    order = [lax.rem(z + d, nz) for d in rs_steps] + [z]
    blocks = [zz * ny + (ny - 1 - y) for zz in order] if ny > 1 else []
    blocks += [zz * ny + y for zz in order]

    def columns(q):
        return pl.ds(pl.multiple_of(q * wide, wide), wide)

    loads = [pltpu.make_async_copy(probes_hbm, probes, in_sem.at[nq])]
    for k, q in enumerate(blocks):
        loads.append(
            pltpu.make_async_copy(integ_hbm.at[:, columns(q)], integ.at[:, columns(q)], in_sem.at[k])
        )
    loads.append(pltpu.make_async_copy(vir_hbm, vir, in_sem.at[nq + 1]))
    small = (
        (occ_hbm, occ), (bocc_hbm, bocc_ref), (bvir_hbm, bvir_ref),
        (bcount_hbm, bcount_ref), (freq_hbm, freq_ref),
    )
    for n, (src, dst) in enumerate(small):
        loads.append(pltpu.make_async_copy(src, dst, in_sem.at[nq + 2 + n]))
    for load in loads:
        load.start()

    barrier = pltpu.get_barrier_semaphore()
    peers = [mate] + ([ymate] if ny > 1 else [])
    peers += [dev(lax.rem(z + d, nz), y, c) for d in range(1, nz)]
    for peer in peers:
        pl.semaphore_signal(barrier, inc=1, device_id=peer, device_id_type=pl.DeviceIdType.MESH)

    sends = []
    core_copies = []
    y_copies = []

    def to_mate(k, q):
        loads[1 + k].wait()
        block = lax.dot_general(
            integ[:, columns(q)], probes[...], (((0,), (0,)), ((), ())),
            preferred_element_type=jnp.float32,
        )
        partial[q] = block.reshape(2, RS_PARTS, LANES // RS_PARTS, LANES)
        if k == 0:
            pl.semaphore_wait(barrier, len(peers))
        copy = remote(partial.at[q, 1 - c], r1.at[q], s1.at[k], v1.at[k], mate)
        copy.start()
        sends.append(copy)
        core_copies.append(copy)

    def to_ymate(k):
        q, zz = blocks[k], order[k]
        core_copies[k].wait_recv()
        for h in range(RS_PARTS):
            partial[q, c, h] = partial[q, c, h] + r1[q, h]
            copy = remote(partial.at[q, c, h], r2.at[zz, h], s2.at[k, h], v2.at[k, h], ymate)
            copy.start()
            sends.append(copy)
            y_copies.append(copy)

    loads[0].wait()
    lag = 2
    n_y = nz if ny > 1 else 0
    for k, q in enumerate(blocks):
        to_mate(k, q)
        if 0 <= k - lag < n_y:
            to_ymate(k - lag)
    for k in range(max(0, nq - lag), n_y):
        to_ymate(k)

    for load in loads[1 + nq:]:
        load.wait()
    gap = vir[pl.ds(bvir_ref[0], 1), :] - occ[bocc_ref[0]]
    omega = freq_ref[0]
    ratio = 2.0 * gap / (gap * gap + omega * omega)
    lane = lax.broadcasted_iota(jnp.int32, (1, LANES), 1)
    ratio = jnp.where(lane < bcount_ref[0], ratio, jnp.zeros_like(ratio))
    weights = jnp.transpose(jnp.broadcast_to(ratio, (LANES, LANES)))

    for d, zz in enumerate(order[:-1]):
        q = blocks[n_y + d]
        core_copies[n_y + d].wait_recv()
        for h in range(RS_PARTS):
            total = partial[q, c, h] + r1[q, h]
            if ny > 1:
                y_copies[d * RS_PARTS + h].wait_recv()
                total = total + r2[zz, h]
            partial[q, c, h] = total
            copy = remote(partial.at[q, c, h], r3.at[z, h], s3.at[d, h], v3.at[z, h], dev(zz, y, c))
            copy.start()
            sends.append(copy)
    core_copies[-1].wait_recv()
    rows_r = LANES // RS_PARTS
    rows_a = LANES // AG_PARTS

    def to_z(h):
        for d in ag_steps:
            zz = lax.rem(z + d, nz)
            copy = remote(
                gathered.at[me, h], gathered.at[me, h], gzs.at[zz, h], gzv.at[z, h], dev(zz, y, c)
            )
            copy.start()
            sends.append(copy)

    def to_y(zs, h):
        j = (zs * ny + y) * 2 + c
        copy = remote(gathered.at[j, h], gathered.at[j, h], gys.at[zs, h], gyv.at[zs, h], ymate)
        copy.start()
        sends.append(copy)

    def spread(zs, yy, h):
        j = (zs * ny + yy) * 2 + c
        q = zs * ny + yy
        copy = remote(gathered.at[j, h], gathered.at[j, h], gcs.at[q, h], gcv.at[q, h], mate)
        copy.start()
        sends.append(copy)

    done = 0
    for h in range(RS_PARTS):
        total = partial[q_me, c, h] + r1[q_me, h]
        if ny > 1:
            y_copies[(nz - 1) * RS_PARTS + h].wait_recv()
            total = total + r2[z, h]
        for d in range(1, nz):
            zs = lax.rem(z + nz - d, nz)
            remote(
                r3.at[zs, h], r3.at[zs, h], s3.at[d - 1, h], v3.at[zs, h], dev(zs, y, c)
            ).wait_recv()
            total = total + r3[zs, h]
        value = (total * weights[h * rows_r:(h + 1) * rows_r]).astype(jnp.bfloat16)
        if rows_a <= rows_r:
            per = rows_r // rows_a
            for g in range(per):
                gathered[me, h * per + g] = value[g * rows_a:(g + 1) * rows_a]
        else:
            per = rows_a // rows_r
            gathered[me, h // per, (h % per) * rows_r:(h % per + 1) * rows_r] = value
        while (done + 1) * rows_a <= (h + 1) * rows_r:
            to_z(done)
            if ny > 1:
                to_y(z, done)
            spread(z, y, done)
            done += 1
    arrivals = [z] + [lax.rem(z + nz - d, nz) for d in ag_steps]
    for h in range(AG_PARTS):
        for zs in arrivals[1:]:
            j = (zs * ny + y) * 2 + c
            remote(
                gathered.at[j, h], gathered.at[j, h], gzs.at[zs, h], gzv.at[zs, h], dev(zs, y, c)
            ).wait_recv()
            if ny > 1:
                to_y(zs, h)
            spread(zs, y, h)
    if ny > 1:
        for h in range(AG_PARTS):
            for zs in arrivals:
                j = (zs * ny + (ny - 1 - y)) * 2 + c
                remote(
                    gathered.at[j, h], gathered.at[j, h], gys.at[zs, h], gyv.at[zs, h], ymate
                ).wait_recv()
                spread(zs, ny - 1 - y, h)

    group = ny * 2 * LANES
    for n, zs in enumerate(arrivals):
        for yy in range(ny):
            q = zs * ny + yy
            j = q * 2 + 1 - c
            for h in range(AG_PARTS):
                remote(
                    gathered.at[j, h], gathered.at[j, h], gcs.at[q, h], gcv.at[q, h], mate
                ).wait_recv()
        rows = gathered[pl.ds(zs * ny * 2, ny * 2)].reshape(group, LANES)
        cols = pl.ds(pl.multiple_of(zs * group, group), group)
        term = jnp.dot(integ[:, cols], rows, preferred_element_type=jnp.float32)
        if n == 0:
            out_ref[...] = term
        else:
            out_ref[...] += term
    for copy in sends:
        copy.wait_send()


def solution(mesh):
    npair = mesh.shape["pair"]
    ny = 2 if npair == 16 else 1
    nz = npair // 2 // ny

    def on_device(integrals, probes, occ, vir, bocc, bvir, bcount, freq):
        aux, ncol = integrals.shape
        nq = nz * ny
        f32, bf16 = jnp.float32, jnp.bfloat16
        vir = vir.reshape(-1, LANES)
        dma = pltpu.SemaphoreType.DMA
        hbm = pl.BlockSpec(memory_space=pltpu.HBM)
        tile_r = (RS_PARTS, LANES // RS_PARTS, LANES)
        tile_a = (AG_PARTS, LANES // AG_PARTS, LANES)
        return pl.pallas_call(
            functools.partial(kernel, nz, ny),
            out_shape=jax.ShapeDtypeStruct((aux, LANES), f32),
            in_specs=[hbm] * 8,
            out_specs=pl.BlockSpec(memory_space=pltpu.VMEM),
            scratch_shapes=[
                pltpu.VMEM((aux, ncol), bf16),
                pltpu.VMEM((aux, LANES), bf16),
                pltpu.VMEM(vir.shape, f32),
                pltpu.SMEM(occ.shape, f32),
                pltpu.SMEM((1,), jnp.int32), pltpu.SMEM((1,), jnp.int32), pltpu.SMEM((1,), jnp.int32),
                pltpu.SMEM((1,), f32),
                pltpu.VMEM((nq, 2) + tile_r, f32),
                pltpu.VMEM((nq,) + tile_r, f32),
                pltpu.VMEM((nz,) + tile_r, f32),
                pltpu.VMEM((nz,) + tile_r, f32),
                pltpu.VMEM((npair,) + tile_a, bf16),
                dma((nq + 7,)),
                dma((nq,)), dma((nq,)),
                dma((nz, RS_PARTS)), dma((nz, RS_PARTS)),
                dma((nz, RS_PARTS)), dma((nz, RS_PARTS)),
                dma((nz, AG_PARTS)), dma((nz, AG_PARTS)),
                dma((nz, AG_PARTS)), dma((nz, AG_PARTS)),
                dma((nq, AG_PARTS)), dma((nq, AG_PARTS)),
            ],
            compiler_params=pltpu.CompilerParams(
                collective_id=0, has_side_effects=True, vmem_limit_bytes=63 * 1024 * 1024
            ),
            cost_estimate=pl.CostEstimate(
                flops=4 * aux * ncol * LANES, bytes_accessed=2 * aux * ncol, transcendentals=0
            ),
        )(integrals, probes, vir, occ, bocc, bvir, bcount, freq)

    in_specs = (
        P("pair", None), P(("groups", "pair"), None), P(), P(),
        P("pair"), P("pair"), P("pair"), P("groups"),
    )
    return jax.shard_map(
        on_device, mesh=mesh, in_specs=in_specs,
        out_specs=P(("groups", "pair"), None), check_vma=False,
    )
```

```python
import functools

import jax
import jax.numpy as jnp
from jax import lax
from jax.experimental import pallas as pl
from jax.experimental.pallas import tpu as pltpu
from jax.sharding import PartitionSpec as P

LANES = 128
RS_PARTS = 2
AG_PARTS = 2


def kernel(
    nz, ny, integ_hbm, probes_hbm, vir_hbm, occ_hbm, bocc_hbm, bvir_hbm, bcount_hbm, freq_hbm,
    out_ref,
    integ, probes, vir, occ, bocc_ref, bvir_ref, bcount_ref, freq_ref, partial, r1, r2, r3, gathered,
    in_sem, s1, v1, s2, v2, s3, v3, gzs, gzv, gys, gyv, gcs, gcv,
):
    nq = nz * ny
    rs_steps = sorted(range(1, nz), key=lambda d: abs(2 * d - nz))
    ag_steps = sorted(range(1, nz), key=lambda d: abs(2 * d - nz))
    me = lax.axis_index("pair")
    c = lax.rem(me, 2)
    q_me = me // 2
    y = lax.rem(q_me, ny)
    z = q_me // ny
    wide = 2 * LANES

    def dev(zz, yy, cc):
        return {"pair": (zz * ny + yy) * 2 + cc}

    mate = dev(z, y, 1 - c)
    ymate = dev(z, ny - 1 - y, c)

    def remote(src, dst, ss, rs, where):
        return pltpu.make_async_remote_copy(
            src_ref=src, dst_ref=dst, send_sem=ss, recv_sem=rs,
            device_id=where, device_id_type=pl.DeviceIdType.MESH,
        )

    order = [lax.rem(z + d, nz) for d in rs_steps] + [z]
    blocks = [zz * ny + (ny - 1 - y) for zz in order] if ny > 1 else []
    blocks += [zz * ny + y for zz in order]

    def columns(q):
        return pl.ds(pl.multiple_of(q * wide, wide), wide)

    loads = [pltpu.make_async_copy(probes_hbm, probes, in_sem.at[nq])]
    for k, q in enumerate(blocks):
        loads.append(
            pltpu.make_async_copy(integ_hbm.at[:, columns(q)], integ.at[:, columns(q)], in_sem.at[k])
        )
    loads.append(pltpu.make_async_copy(vir_hbm, vir, in_sem.at[nq + 1]))
    small = (
        (occ_hbm, occ), (bocc_hbm, bocc_ref), (bvir_hbm, bvir_ref),
        (bcount_hbm, bcount_ref), (freq_hbm, freq_ref),
    )
    for n, (src, dst) in enumerate(small):
        loads.append(pltpu.make_async_copy(src, dst, in_sem.at[nq + 2 + n]))
    for load in loads:
        load.start()

    barrier = pltpu.get_barrier_semaphore()
    peers = [mate] + ([ymate] if ny > 1 else [])
    peers += [dev(lax.rem(z + d, nz), y, c) for d in range(1, nz)]
    for peer in peers:
        pl.semaphore_signal(barrier, inc=1, device_id=peer, device_id_type=pl.DeviceIdType.MESH)

    sends = []
    core_copies = []
    y_copies = []

    def to_mate(k, q):
        loads[1 + k].wait()
        block = lax.dot_general(
            integ[:, columns(q)], probes[...], (((0,), (0,)), ((), ())),
            preferred_element_type=jnp.float32,
        )
        partial[q] = block.reshape(2, RS_PARTS, LANES // RS_PARTS, LANES)
        if k == 0:
            pl.semaphore_wait(barrier, len(peers))
        copy = remote(partial.at[q, 1 - c], r1.at[q], s1.at[k], v1.at[k], mate)
        copy.start()
        sends.append(copy)
        core_copies.append(copy)

    def to_ymate(k):
        q, zz = blocks[k], order[k]
        core_copies[k].wait_recv()
        for h in range(RS_PARTS):
            partial[q, c, h] = partial[q, c, h] + r1[q, h]
            copy = remote(partial.at[q, c, h], r2.at[zz, h], s2.at[k, h], v2.at[k, h], ymate)
            copy.start()
            sends.append(copy)
            y_copies.append(copy)

    loads[0].wait()
    lag = 2
    n_y = nz if ny > 1 else 0
    for k, q in enumerate(blocks):
        to_mate(k, q)
        if 0 <= k - lag < n_y:
            to_ymate(k - lag)
    for k in range(max(0, nq - lag), n_y):
        to_ymate(k)

    for load in loads[1 + nq:]:
        load.wait()
    gap = vir[pl.ds(bvir_ref[0], 1), :] - occ[bocc_ref[0]]
    omega = freq_ref[0]
    ratio = 2.0 * gap / (gap * gap + omega * omega)
    lane = lax.broadcasted_iota(jnp.int32, (1, LANES), 1)
    ratio = jnp.where(lane < bcount_ref[0], ratio, jnp.zeros_like(ratio))
    weights = jnp.transpose(jnp.broadcast_to(ratio, (LANES, LANES)))

    for d, zz in enumerate(order[:-1]):
        q = blocks[n_y + d]
        core_copies[n_y + d].wait_recv()
        for h in range(RS_PARTS):
            total = partial[q, c, h] + r1[q, h]
            if ny > 1:
                y_copies[d * RS_PARTS + h].wait_recv()
                total = total + r2[zz, h]
            partial[q, c, h] = total
            copy = remote(partial.at[q, c, h], r3.at[z, h], s3.at[d, h], v3.at[z, h], dev(zz, y, c))
            copy.start()
            sends.append(copy)
    core_copies[-1].wait_recv()
    rows_r = LANES // RS_PARTS
    rows_a = LANES // AG_PARTS

    def to_z(h):
        for d in ag_steps:
            zz = lax.rem(z + d, nz)
            copy = remote(
                gathered.at[me, h], gathered.at[me, h], gzs.at[zz, h], gzv.at[z, h], dev(zz, y, c)
            )
            copy.start()
            sends.append(copy)

    def to_y(zs, h):
        j = (zs * ny + y) * 2 + c
        copy = remote(gathered.at[j, h], gathered.at[j, h], gys.at[zs, h], gyv.at[zs, h], ymate)
        copy.start()
        sends.append(copy)

    def spread(zs, yy, h):
        j = (zs * ny + yy) * 2 + c
        q = zs * ny + yy
        copy = remote(gathered.at[j, h], gathered.at[j, h], gcs.at[q, h], gcv.at[q, h], mate)
        copy.start()
        sends.append(copy)

    done = 0
    for h in range(RS_PARTS):
        total = partial[q_me, c, h] + r1[q_me, h]
        if ny > 1:
            y_copies[(nz - 1) * RS_PARTS + h].wait_recv()
            total = total + r2[z, h]
        for d in range(1, nz):
            zs = lax.rem(z + nz - d, nz)
            remote(
                r3.at[zs, h], r3.at[zs, h], s3.at[d - 1, h], v3.at[zs, h], dev(zs, y, c)
            ).wait_recv()
            total = total + r3[zs, h]
        value = (total * weights[h * rows_r:(h + 1) * rows_r]).astype(jnp.bfloat16)
        if rows_a <= rows_r:
            per = rows_r // rows_a
            for g in range(per):
                gathered[me, h * per + g] = value[g * rows_a:(g + 1) * rows_a]
        else:
            per = rows_a // rows_r
            gathered[me, h // per, (h % per) * rows_r:(h % per + 1) * rows_r] = value
        while (done + 1) * rows_a <= (h + 1) * rows_r:
            if ny > 1:
                to_y(z, done)
            to_z(done)
            spread(z, y, done)
            done += 1
    arrivals = [z] + [lax.rem(z + nz - d, nz) for d in ag_steps]
    for h in range(AG_PARTS):
        for zs in arrivals[1:]:
            j = (zs * ny + y) * 2 + c
            remote(
                gathered.at[j, h], gathered.at[j, h], gzs.at[zs, h], gzv.at[zs, h], dev(zs, y, c)
            ).wait_recv()
            if ny > 1:
                to_y(zs, h)
            spread(zs, y, h)
    if ny > 1:
        for h in range(AG_PARTS):
            for zs in arrivals:
                j = (zs * ny + (ny - 1 - y)) * 2 + c
                remote(
                    gathered.at[j, h], gathered.at[j, h], gys.at[zs, h], gyv.at[zs, h], ymate
                ).wait_recv()
                spread(zs, ny - 1 - y, h)

    group = ny * 2 * LANES
    for n, zs in enumerate(arrivals):
        for yy in range(ny):
            q = zs * ny + yy
            j = q * 2 + 1 - c
            for h in range(AG_PARTS):
                remote(
                    gathered.at[j, h], gathered.at[j, h], gcs.at[q, h], gcv.at[q, h], mate
                ).wait_recv()
        rows = gathered[pl.ds(zs * ny * 2, ny * 2)].reshape(group, LANES)
        cols = pl.ds(pl.multiple_of(zs * group, group), group)
        term = jnp.dot(integ[:, cols], rows, preferred_element_type=jnp.float32)
        if n == 0:
            out_ref[...] = term
        else:
            out_ref[...] += term
    for copy in sends:
        copy.wait_send()


def solution(mesh):
    npair = mesh.shape["pair"]
    ny = 2 if npair == 16 else 1
    nz = npair // 2 // ny

    def on_device(integrals, probes, occ, vir, bocc, bvir, bcount, freq):
        aux, ncol = integrals.shape
        nq = nz * ny
        f32, bf16 = jnp.float32, jnp.bfloat16
        vir = vir.reshape(-1, LANES)
        dma = pltpu.SemaphoreType.DMA
        hbm = pl.BlockSpec(memory_space=pltpu.HBM)
        tile_r = (RS_PARTS, LANES // RS_PARTS, LANES)
        tile_a = (AG_PARTS, LANES // AG_PARTS, LANES)
        return pl.pallas_call(
            functools.partial(kernel, nz, ny),
            out_shape=jax.ShapeDtypeStruct((aux, LANES), f32),
            in_specs=[hbm] * 8,
            out_specs=pl.BlockSpec(memory_space=pltpu.VMEM),
            scratch_shapes=[
                pltpu.VMEM((aux, ncol), bf16),
                pltpu.VMEM((aux, LANES), bf16),
                pltpu.VMEM(vir.shape, f32),
                pltpu.SMEM(occ.shape, f32),
                pltpu.SMEM((1,), jnp.int32), pltpu.SMEM((1,), jnp.int32), pltpu.SMEM((1,), jnp.int32),
                pltpu.SMEM((1,), f32),
                pltpu.VMEM((nq, 2) + tile_r, f32),
                pltpu.VMEM((nq,) + tile_r, f32),
                pltpu.VMEM((nz,) + tile_r, f32),
                pltpu.VMEM((nz,) + tile_r, f32),
                pltpu.VMEM((npair,) + tile_a, bf16),
                dma((nq + 7,)),
                dma((nq,)), dma((nq,)),
                dma((nz, RS_PARTS)), dma((nz, RS_PARTS)),
                dma((nz, RS_PARTS)), dma((nz, RS_PARTS)),
                dma((nz, AG_PARTS)), dma((nz, AG_PARTS)),
                dma((nz, AG_PARTS)), dma((nz, AG_PARTS)),
                dma((nq, AG_PARTS)), dma((nq, AG_PARTS)),
            ],
            compiler_params=pltpu.CompilerParams(
                collective_id=0, has_side_effects=True, vmem_limit_bytes=63 * 1024 * 1024
            ),
            cost_estimate=pl.CostEstimate(
                flops=4 * aux * ncol * LANES, bytes_accessed=2 * aux * ncol, transcendentals=0
            ),
        )(integrals, probes, vir, occ, bocc, bvir, bcount, freq)

    in_specs = (
        P("pair", None), P(("groups", "pair"), None), P(), P(),
        P("pair"), P("pair"), P("pair"), P("groups"),
    )
    return jax.shard_map(
        on_device, mesh=mesh, in_specs=in_specs,
        out_specs=P(("groups", "pair"), None), check_vma=False,
    )
```
